512 devices in a mesh: dp: 4 (over x), vocab: 128 (over z, y, core).
Axes of the slice: x: 4, y: 4, z: 16, core: 2. Of those that a mesh axis runs over, the one named last changes fastest.
Arguments:
- hidden_states: bfloat16 [512, 4096], P('dp', 'vocab'), may hold values from -6 to 6
- teacher_logprob: bfloat16 [512, 131072], P(('dp', 'vocab')), may hold values from -12 to -0.5
- head_weight: bfloat16 [4096, 131072], P('dp', 'vocab'), may hold values from -6 to 6
- token_ids: int32 [512], P('dp'), may hold values from 0 to 131071
- padding_mask: int32 [512], P('dp'), may hold values 0 or 1
Outputs:
- logit_grad: bfloat16 [512, 131072], P('dp', 'vocab')
- hidden_grad: float32 [512, 4096], P('dp', 'vocab')
- head_grad: bfloat16 [4096, 131072], P('dp', 'vocab')
The draws below stay inside these ranges and needn't reach their ends.
All inputs are finite; a program needn't handle non-finite values. No bound on the sum of `padding_mask` on one device may be relied on, other than what follows from the above.
Results may differ from the reference program's by a relative error of at most 0.012.
Values may be sent and summed in bfloat16 or wider, within the bound.
No kernel may reach another device: no remote copies, remote signals or barrier semaphores. Data moves between devices by JAX's collectives and lax.ppermute only.
A program may use at most 64 MiB of HBM per device.

```python
import math
import jax
import jax.numpy as jnp
import numpy as np
from jax import lax

D = 4096
TOK_DEV = 128
TOKENS = 512
V = 131072


def hidden_rows(key, row_spread):
    key_normal = jax.random.fold_in(jax.random.fold_in(key, 11), 0)
    key_scale = jax.random.fold_in(jax.random.fold_in(key, 11), 2)
    normal_part = jnp.clip(jax.random.normal(key_normal, (TOKENS, D), jnp.float32), -6.0, 6.0)
    base = normal_part
    scales = jnp.exp(row_spread * jax.random.uniform(key_scale, (TOKENS, 1), jnp.float32, -1.0, 1.0))
    return (base, scales)


def draw_hidden_states(key, part):
    rows, scales = hidden_rows(key, 0.0)
    return rows.astype(jnp.bfloat16)


def draw_head_weight(key, part):
    rows, scales = hidden_rows(key, 0.0)
    strength = 0.0
    key = jax.random.fold_in(key, 5)
    key_entries, key_scale, key_pick, key_first, key_second, key_gap = jax.random.split(key, 6)
    ramp = jnp.exp(0.2623643 * jnp.arange(V, dtype=jnp.float32) / V)
    column_scale = jnp.exp(jax.random.uniform(key_scale, (1, V), jnp.float32, -0.2876821, 2.014903)) * ramp[None, :]
    entries = jnp.clip(jax.random.normal(key_entries, (D, V), jnp.float32), -6.0, 6.0) * column_scale / D ** 0.5
    picked = jax.random.randint(key_pick, (6,), 0, TOKENS)
    first_cols = jax.random.randint(key_first, (6,), 0, V)
    second_cols = jax.random.randint(key_second, (6,), 0, V)
    levels = jnp.array([110.0, 160.0, 230.0, 300.0, 140.0, 260.0], jnp.float32)
    gaps = jax.random.uniform(key_gap, (6,), jnp.float32, 1.0, 3.0)
    aligned = rows[picked] / (D * scales[picked] ** 2)
    entries = entries.at[:, first_cols].add(strength * (aligned * levels[:, None]).T)
    entries = entries.at[:, second_cols].add(strength * (aligned * (levels - gaps)[:, None]).T)
    return entries.astype(jnp.bfloat16)


def place_ends(values, key, low, top_value):
    extent = values.shape
    place = [jax.random.randint(jax.random.fold_in(key, axis), (), 0, extent[axis]) for axis in range(len(extent))]
    values = values.at[tuple(place)].set(low)
    longest = extent.index(max(extent))
    place[longest] = (place[longest] + 1) % extent[longest]
    return values.at[tuple(place)].set(top_value)


def block_levels(stream_key, dims, pieces, low, top_value):
    loudness, own = 1.0, jax.random.fold_in(stream_key, 6)
    for position, blocks in pieces:
        heights = jnp.exp(jax.random.uniform(jax.random.fold_in(own, position), (blocks,), jnp.float32, low / len(pieces), top_value / len(pieces)))
        loudness = loudness * jnp.repeat(heights, dims[position] // blocks).reshape([-1 if axis == position else 1 for axis in range(len(dims))])
    return loudness


def ranked_wide(rng, shape, count, lean):
    weights = [min(1 << octave, count + 1 - (1 << octave)) * (1 << 20) // math.isqrt((1 << octave) ** lean) + 1 for octave in range((count + 1).bit_length()) if 1 << octave <= count]
    scale = 1 + sum(weights) // (1 << 30)
    grid = np.cumsum(np.array([max(1, weight // scale) for weight in weights]))
    ticket = jax.random.randint(jax.random.fold_in(rng, 1), shape, 0, int(grid[len(weights) - 1]))
    start = jnp.left_shift(1, jnp.searchsorted(jnp.asarray(grid, jnp.int32), ticket, side="right").astype(jnp.int32))
    standing = start - 1 + jax.random.randint(jax.random.fold_in(rng, 4), shape, 0, 1 << 30) % jnp.minimum(start, count + 1 - start)
    return jax.random.permutation(jax.random.fold_in(rng, 2), count)[standing].astype(jnp.int32)


def setup_inputs(seed: int = 0) -> dict:
    key_of = jax.random.split(jax.random.key(seed), 6)
    hidden_states = draw_hidden_states(jax.random.fold_in(key_of[5], 71), 0)
    teacher_logprob = jnp.clip(-12.0 + 11.5 * jax.random.uniform(key_of[1], (TOKENS, V), jnp.float32) ** block_levels(key_of[1], (TOKENS, V), ((0, 512),), -0.2, 0.2), -12.0, -0.5).astype(jnp.bfloat16)
    head_weight = draw_head_weight(jax.random.fold_in(key_of[5], 71), 0)
    token_ids = place_ends(ranked_wide(key_of[3], (TOKENS,), V, 2), jax.random.fold_in(key_of[3], 3), 0, V - 1).astype(jnp.int32)
    padding_mask = place_ends((jax.random.randint(key_of[4], (TOKENS,), 0, 8) < 7).astype(jnp.int32), jax.random.fold_in(key_of[4], 1), 0, 1)
    return dict(hidden_states=hidden_states, teacher_logprob=teacher_logprob, head_weight=head_weight, token_ids=token_ids, padding_mask=padding_mask)


anchor_weight = 0.25


def reference(hidden_states, teacher_logprob, head_weight, token_ids, padding_mask):
    rows_total = hidden_states.shape[0]
    width = hidden_states.shape[1]
    vocab = head_weight.shape[1]
    blocks = rows_total // TOK_DEV
    columns = jnp.arange(vocab, dtype=jnp.int32)

    def one_block(carry, index):
        start = (index * TOK_DEV).astype(jnp.int32)
        hidden = lax.dynamic_slice_in_dim(hidden_states, start, TOK_DEV, 0)
        teacher = lax.dynamic_slice_in_dim(teacher_logprob, start, TOK_DEV, 0).astype(jnp.float32)
        ids = lax.dynamic_slice_in_dim(token_ids, start, TOK_DEV, 0)
        keep = lax.dynamic_slice_in_dim(padding_mask, start, TOK_DEV, 0).astype(jnp.float32)
        logits = jnp.dot(hidden, head_weight, preferred_element_type=jnp.float32)
        top = jnp.max(logits, axis=1, keepdims=True)
        expo = jnp.exp(logits - top)
        total = jnp.sum(expo, axis=1, keepdims=True)
        gap = logits - teacher
        weighted = jnp.sum(expo * gap, axis=1, keepdims=True)
        prob = expo / total
        onehot = (columns[None, :] == ids[:, None]).astype(jnp.float32)
        grad = keep[:, None] * (prob * (gap - weighted / total) + anchor_weight * (prob - onehot))
        grad = grad.astype(jnp.bfloat16)
        back = lax.dot_general(grad, head_weight, (((1,), (1,)), ((), ())), preferred_element_type=jnp.float32)
        return carry, (grad, back)

    unused, outputs = lax.scan(one_block, jnp.zeros((), jnp.float32), jnp.arange(blocks, dtype=jnp.int32))
    logit_grad = outputs[0].reshape(rows_total, vocab)
    hidden_grad = outputs[1].reshape(rows_total, width)
    block_width = width // 8

    def weight_rows(index):
        start = (index * block_width).astype(jnp.int32)
        piece = lax.dynamic_slice_in_dim(hidden_states, start, block_width, 1)
        product = lax.dot_general(piece, logit_grad, (((0,), (0,)), ((), ())), preferred_element_type=jnp.float32)
        return product.astype(jnp.bfloat16)

    head_grad = lax.map(weight_rows, jnp.arange(8, dtype=jnp.int32)).reshape(width, vocab)
    return logit_grad, hidden_grad, head_grad
```

```python
import jax
import jax.numpy as jnp
from jax import lax
from jax.sharding import Mesh, PartitionSpec as P

anchor_weight = 0.25

X, Z, Y, C = 4, 16, 4, 2
K = Z // X
TOK = 128
FEAT = 32
ROWS = 1024
COLS = 1024

f32 = jnp.float32
bf16 = jnp.bfloat16


def shift(value, axis, size, step):
    return lax.ppermute(value, axis, [(i, (i + step) % size) for i in range(size)])


def spread(value, axes, size):
    sent = jnp.broadcast_to(value[None], (size,) + value.shape)
    return lax.all_to_all(sent, axes, 0, 0, tiled=True)


def merge(parts):
    top = jnp.max(parts[:, 0], axis=0)
    scale = jnp.exp(parts[:, 0] - top[None])
    return jnp.stack(
        [top, jnp.sum(scale * parts[:, 1], axis=0), jnp.sum(scale * parts[:, 2], axis=0)]
    )


def gather_hidden(hidden_states):
    mine = spread(hidden_states.T, "z", Z)
    sent = jnp.broadcast_to(mine.reshape(X, 1, K, FEAT, TOK), (X, Y, K, FEAT, TOK))
    here = lax.all_to_all(sent.reshape(X * Y, K, FEAT, TOK), ("x", "y"), 0, 0, tiled=True)
    there = shift(here, "c", C, 1)
    first = lax.axis_index("c") == 0
    both = jnp.stack([jnp.where(first, here, there), jnp.where(first, there, here)])
    both = both.reshape(C, X, Y, K, FEAT, TOK)
    return both.transpose(1, 3, 2, 0, 4, 5).reshape(X, ROWS, TOK)


def local(hidden_states, teacher_logprob, head_weight, token_ids, padding_mask):
    me = lax.axis_index("x")
    hidden = gather_hidden(hidden_states)
    partial = lax.dot_general(
        hidden, head_weight, (((1,), (0,)), ((), ())), preferred_element_type=f32
    )
    logits = lax.dynamic_index_in_dim(partial, me, 0, keepdims=False)
    for step in (2, 1, 3):
        chunk = lax.dynamic_index_in_dim(partial, lax.rem(me + step, X), 0, keepdims=False)
        logits = logits + shift(chunk, "x", X, step)

    teacher = lax.all_to_all(
        teacher_logprob, ("z", "y", "c"), split_axis=1, concat_axis=0, tiled=True
    )
    gap = logits - teacher.astype(f32)
    top = jnp.max(logits, axis=1)
    expo = jnp.exp(logits - top[:, None])
    stats = jnp.stack([top, jnp.sum(expo, axis=1), jnp.sum(expo * gap, axis=1)])
    stats = merge(spread(stats, ("y", "c"), Y * C))
    stats = merge(spread(stats, "z", Z))
    whole, total, weighted = stats[0], stats[1], stats[2]

    start = (
        (lax.axis_index("z") * Y + lax.axis_index("y")) * C + lax.axis_index("c")
    ) * COLS
    columns = start + jnp.arange(COLS, dtype=jnp.int32)
    onehot = (columns[None, :] == token_ids[:, None]).astype(f32)
    prob = jnp.exp(logits - whole[:, None]) / total[:, None]
    keep = padding_mask.astype(f32)[:, None]
    logit_grad = (
        keep * (prob * (gap - (weighted / total)[:, None]) + anchor_weight * (prob - onehot))
    ).astype(bf16)

    grads = spread(logit_grad, "x", X).reshape(X * TOK, COLS)
    feature = lax.dot_general(
        head_weight, grads, (((1,), (1,)), ((), ())), preferred_element_type=f32
    ).astype(bf16)
    feature = feature.reshape(K, Y, C, FEAT, X, TOK)
    cme = lax.axis_index("c")
    sent = lax.dynamic_index_in_dim(feature, 1 - cme, 2, keepdims=False)
    kept = lax.dynamic_index_in_dim(feature, cme, 2, keepdims=False)
    pair = kept.astype(f32) + shift(sent, "c", C, 1).astype(f32)
    pair = pair.astype(bf16).transpose(3, 1, 0, 2, 4).reshape(X * Y, K, FEAT, TOK)
    plane = lax.all_to_all(pair, ("x", "y"), 0, 0, tiled=True)
    plane = jnp.sum(plane.reshape(X, Y, K, FEAT, TOK).astype(f32), axis=1).astype(bf16)
    line = lax.all_to_all(plane.reshape(Z, FEAT, TOK), "z", 0, 0, tiled=True)
    hidden_grad = jnp.sum(line.astype(f32), axis=0).T

    head_grad = lax.dot_general(
        hidden.transpose(1, 0, 2).reshape(ROWS, X * TOK),
        grads,
        (((1,), (0,)), ((), ())),
        preferred_element_type=f32,
    ).astype(bf16)
    return (logit_grad, hidden_grad, head_grad)


def solution(mesh):
    inner = Mesh(mesh.devices.reshape(X, Z, Y, C), ("x", "z", "y", "c"))
    v = ("z", "y", "c")
    in_specs = (P("x", v), P(("x",) + v, None), P("x", v), P("x"), P("x"))
    out_specs = (P("x", v), P("x", v), P("x", v))
    return jax.shard_map(local, mesh=inner, in_specs=in_specs, out_specs=out_specs, check_vma=False)
```

```python
import jax
import jax.numpy as jnp
from jax import lax
from jax.experimental import pallas as pl
from jax.experimental.pallas import tpu as pltpu
from jax.sharding import Mesh, PartitionSpec as P

anchor_weight = 0.25

X, Z, Y, C = 4, 16, 4, 2
K = Z // X
TOK = 128
FEAT = 32
ROWS = 1024
COLS = 1024
ADD_COST = 6 * 10**9
LIMIT = 48 * 1024 * 1024

f32 = jnp.float32
bf16 = jnp.bfloat16
STEPS = (2, 1, 3, 0)


def shift(value, axis, size, step):
    return lax.ppermute(value, axis, [(i, (i + step) % size) for i in range(size)])


def spread(value, axes, size):
    sent = jnp.broadcast_to(value[None], (size,) + value.shape)
    return lax.all_to_all(sent, axes, 0, 0, tiled=True)


def merge(parts):
    top = jnp.max(parts[:, 0], axis=0)
    scale = jnp.exp(parts[:, 0] - top[None])
    return jnp.stack(
        [top, jnp.sum(scale * parts[:, 1], axis=0), jnp.sum(scale * parts[:, 2], axis=0)]
    )


def gather_hidden(hidden_states):
    mine = spread(hidden_states.T, "z", Z)
    sent = jnp.broadcast_to(mine.reshape(X, 1, K, FEAT, TOK), (X, Y, K, FEAT, TOK))
    here = lax.all_to_all(sent.reshape(X * Y, K, FEAT, TOK), ("x", "y"), 0, 0, tiled=True)
    return here, shift(here, "c", C, 1)


def partial_kernel(place, here, there, head, far, up, down, own, hidden_t, lhs):
    me, core = place[0], place[1]
    outs = (far, up, down, own)
    for t in range(X):
        for k in range(K):
            for y in range(Y):
                row = (k * Y + y) * C * FEAT
                for mine, ref in ((core, here), (1 - core, there)):
                    at = pl.ds(pl.multiple_of(row + mine * FEAT, FEAT), FEAT)
                    piece = ref[t * Y + y, k]
                    lhs[t, at, :] = piece
                    hidden_t[at, t * TOK : (t + 1) * TOK] = piece
    for step, out in zip(STEPS, outs):
        t = lax.rem(me + step, X)
        out[...] = lax.dot_general(
            lhs[t], head[...], (((0,), (0,)), ((), ())), preferred_element_type=f32
        )


def partial_logits(place, here, there, head):
    vmem = pl.BlockSpec(memory_space=pltpu.VMEM)
    chunk = jax.ShapeDtypeStruct((TOK, COLS), f32)
    return pl.pallas_call(
        partial_kernel,
        out_shape=(chunk,) * X + (jax.ShapeDtypeStruct((ROWS, X * TOK), bf16),),
        in_specs=[pl.BlockSpec(memory_space=pltpu.SMEM), vmem, vmem, vmem],
        out_specs=(vmem,) * (X + 1),
        scratch_shapes=[pltpu.VMEM((X, ROWS, TOK), bf16)],
        compiler_params=pltpu.CompilerParams(vmem_limit_bytes=LIMIT),
        cost_estimate=pl.CostEstimate(
            flops=2 * X * TOK * ROWS * COLS, bytes_accessed=6 << 20, transcendentals=0
        ),
        name="partial_logits",
    )(place, here, there, head)


def add_kernel(own, far, total):
    total[...] = own[...] + far[...]


def add_far(own, far):
    rows = pl.BlockSpec((TOK // 2, COLS), lambda i: (i, 0))
    return pl.pallas_call(
        add_kernel,
        out_shape=jax.ShapeDtypeStruct((TOK, COLS), f32),
        grid=(2,),
        in_specs=[rows, rows],
        out_specs=rows,
        compiler_params=pltpu.CompilerParams(vmem_limit_bytes=LIMIT),
        cost_estimate=pl.CostEstimate(flops=ADD_COST, bytes_accessed=3 << 19, transcendentals=0),
        name="add_far",
    )(own, far)


def feature_kernel(place, grads, head, sent, kept):
    first = place[1] == 0
    band = Y * C * FEAT
    for k in range(K):
        part = lax.dot_general(
            head[k * band : (k + 1) * band, :],
            grads[...],
            (((1,), (1,)), ((), ())),
            preferred_element_type=f32,
        )
        for y in range(Y):
            low = part[y * C * FEAT : y * C * FEAT + FEAT]
            high = part[y * C * FEAT + FEAT : (y + 1) * C * FEAT]
            keep = jnp.where(first, low, high)
            give = jnp.where(first, high, low).astype(bf16)
            for t in range(X):
                kept[t * Y + y, k] = keep[:, t * TOK : (t + 1) * TOK]
                sent[t * Y + y, k] = give[:, t * TOK : (t + 1) * TOK]


def feature_parts(place, grads, head):
    vmem = pl.BlockSpec(memory_space=pltpu.VMEM)
    shape = (X * Y, K, FEAT, TOK)
    return pl.pallas_call(
        feature_kernel,
        out_shape=(jax.ShapeDtypeStruct(shape, bf16), jax.ShapeDtypeStruct(shape, f32)),
        in_specs=[pl.BlockSpec(memory_space=pltpu.SMEM), vmem, vmem],
        out_specs=(vmem, vmem),
        compiler_params=pltpu.CompilerParams(vmem_limit_bytes=LIMIT),
        cost_estimate=pl.CostEstimate(
            flops=2 * X * TOK * ROWS * COLS, bytes_accessed=5 << 20, transcendentals=0
        ),
        name="feature_parts",
    )(place, grads, head)


def local(hidden_states, teacher_logprob, head_weight, token_ids, padding_mask):
    place = jnp.stack([lax.axis_index("x"), lax.axis_index("c")]).astype(jnp.int32)
    here, there = gather_hidden(hidden_states)
    teacher = teacher_logprob.reshape(Z * Y * C, 2, COLS // 2)
    teacher, there = lax.optimization_barrier((teacher, there))
    far, up, down, own, hidden_t = partial_logits(place, here, there, head_weight)
    teacher, own = lax.optimization_barrier((teacher, own))
    teacher = lax.all_to_all(teacher, ("z", "y", "c"), 0, 0, tiled=True).reshape(TOK, COLS)
    logits = add_far(own, shift(far, "x", X, 2)) + (shift(up, "x", X, 1) + shift(down, "x", X, 3))
    gap = logits - teacher.astype(f32)
    top = jnp.max(logits, axis=1)
    expo = jnp.exp(logits - top[:, None])
    stats = jnp.stack([top, jnp.sum(expo, axis=1), jnp.sum(expo * gap, axis=1)])
    stats = merge(spread(stats, ("y", "c"), Y * C))
    stats = merge(spread(stats, "z", Z))
    whole, total, weighted = stats[0], stats[1], stats[2]

    start = (
        (lax.axis_index("z") * Y + lax.axis_index("y")) * C + lax.axis_index("c")
    ) * COLS
    columns = start + jnp.arange(COLS, dtype=jnp.int32)
    onehot = (columns[None, :] == token_ids[:, None]).astype(f32)
    prob = jnp.exp(logits - whole[:, None]) / total[:, None]
    keep = padding_mask.astype(f32)[:, None]
    logit_grad = (
        keep * (prob * (gap - (weighted / total)[:, None]) + anchor_weight * (prob - onehot))
    ).astype(bf16)

    grads = spread(logit_grad, "x", X).reshape(X * TOK, COLS)
    sent, kept = feature_parts(place, grads, head_weight)
    pair = (kept + shift(sent, "c", C, 1).astype(f32)).astype(bf16)
    plane = lax.all_to_all(pair, ("x", "y"), 0, 0, tiled=True)
    plane = jnp.sum(plane.reshape(X, Y, K, FEAT, TOK).astype(f32), axis=1).astype(bf16)
    line = lax.all_to_all(plane.reshape(Z, FEAT, TOK), "z", 0, 0, tiled=True)
    hidden_grad = jnp.sum(line.astype(f32), axis=0).T

    head_grad = jnp.dot(hidden_t, grads, preferred_element_type=f32).astype(bf16)
    return (logit_grad, hidden_grad, head_grad)


def solution(mesh):
    inner = Mesh(mesh.devices.reshape(X, Z, Y, C), ("x", "z", "y", "c"))
    v = ("z", "y", "c")
    in_specs = (P("x", v), P(("x",) + v, None), P("x", v), P("x"), P("x"))
    out_specs = (P("x", v), P("x", v), P("x", v))
    return jax.shard_map(local, mesh=inner, in_specs=in_specs, out_specs=out_specs, check_vma=False)
```

```python
import jax
import jax.numpy as jnp
from jax import lax
from jax.experimental import pallas as pl
from jax.experimental.pallas import tpu as pltpu
from jax.sharding import Mesh, PartitionSpec as P

anchor_weight = 0.25

X, Z, Y, C = 4, 16, 4, 2
K = Z // X
TOK = 128
FEAT = 32
ROWS = 1024
COLS = 1024
ADD_COST = 6 * 10**9
LIMIT = 48 * 1024 * 1024

f32 = jnp.float32
bf16 = jnp.bfloat16
STEPS = (2, 1, 3, 0)


def shift(value, axis, size, step):
    return lax.ppermute(value, axis, [(i, (i + step) % size) for i in range(size)])


def spread(value, axes, size):
    sent = jnp.broadcast_to(value[None], (size,) + value.shape)
    return lax.all_to_all(sent, axes, 0, 0, tiled=True)


def merge(parts):
    top = jnp.max(parts[:, 0], axis=0)
    scale = jnp.exp(parts[:, 0] - top[None])
    return jnp.stack(
        [top, jnp.sum(scale * parts[:, 1], axis=0), jnp.sum(scale * parts[:, 2], axis=0)]
    )


def gather_hidden(hidden_states):
    mine = spread(hidden_states.T, "z", Z)
    sent = jnp.broadcast_to(mine.reshape(X, 1, K, FEAT, TOK), (X, Y, K, FEAT, TOK))
    here = lax.all_to_all(sent.reshape(X * Y, K, FEAT, TOK), ("x", "y"), 0, 0, tiled=True)
    return here, shift(here, "c", C, 1)


def partial_kernel(place, here, there, head, far, up, down, own, hidden_t, lhs, flat, sem):
    me, core = place[0], place[1]
    outs = (far, up, down, own)
    for t in range(X):
        for k in range(K):
            for y in range(Y):
                row = (k * Y + y) * C * FEAT
                for mine, ref in ((core, here), (1 - core, there)):
                    at = pl.ds(pl.multiple_of(row + mine * FEAT, FEAT), FEAT)
                    piece = ref[t * Y + y, k]
                    lhs[t, at, :] = piece
                    flat[at, t * TOK : (t + 1) * TOK] = piece
    save = pltpu.make_async_copy(flat, hidden_t, sem)
    save.start()
    for step, out in zip(STEPS, outs):
        t = lax.rem(me + step, X)
        out[...] = lax.dot_general(
            lhs[t], head[...], (((0,), (0,)), ((), ())), preferred_element_type=f32
        )
    save.wait()


def partial_logits(place, here, there, head):
    vmem = pl.BlockSpec(memory_space=pltpu.VMEM)
    chunk = jax.ShapeDtypeStruct((TOK, COLS), f32)
    return pl.pallas_call(
        partial_kernel,
        out_shape=(chunk,) * X + (jax.ShapeDtypeStruct((ROWS, X * TOK), bf16),),
        in_specs=[pl.BlockSpec(memory_space=pltpu.SMEM), vmem, vmem, vmem],
        out_specs=(vmem,) * X + (pl.BlockSpec(memory_space=pl.ANY),),
        scratch_shapes=[
            pltpu.VMEM((X, ROWS, TOK), bf16),
            pltpu.VMEM((ROWS, X * TOK), bf16),
            pltpu.SemaphoreType.DMA,
        ],
        compiler_params=pltpu.CompilerParams(vmem_limit_bytes=LIMIT),
        cost_estimate=pl.CostEstimate(
            flops=2 * X * TOK * ROWS * COLS, bytes_accessed=6 << 20, transcendentals=0
        ),
        name="partial_logits",
    )(place, here, there, head)


def add_kernel(own, far, total):
    total[...] = own[...] + far[...]


def add_far(own, far):
    rows = pl.BlockSpec((TOK // 2, COLS), lambda i: (i, 0))
    return pl.pallas_call(
        add_kernel,
        out_shape=jax.ShapeDtypeStruct((TOK, COLS), f32),
        grid=(2,),
        in_specs=[rows, rows],
        out_specs=rows,
        compiler_params=pltpu.CompilerParams(vmem_limit_bytes=LIMIT),
        cost_estimate=pl.CostEstimate(flops=ADD_COST, bytes_accessed=3 << 19, transcendentals=0),
        name="add_far",
    )(own, far)


def feature_kernel(place, grads, head, sent, kept):
    first = place[1] == 0
    band = Y * C * FEAT
    for k in range(K):
        part = lax.dot_general(
            head[k * band : (k + 1) * band, :],
            grads[...],
            (((1,), (1,)), ((), ())),
            preferred_element_type=f32,
        )
        for y in range(Y):
            low = part[y * C * FEAT : y * C * FEAT + FEAT]
            high = part[y * C * FEAT + FEAT : (y + 1) * C * FEAT]
            keep = jnp.where(first, low, high)
            give = jnp.where(first, high, low).astype(bf16)
            for t in range(X):
                kept[t * Y + y, k] = keep[:, t * TOK : (t + 1) * TOK]
                sent[t * Y + y, k] = give[:, t * TOK : (t + 1) * TOK]


def feature_parts(place, grads, head):
    vmem = pl.BlockSpec(memory_space=pltpu.VMEM)
    shape = (X * Y, K, FEAT, TOK)
    return pl.pallas_call(
        feature_kernel,
        out_shape=(jax.ShapeDtypeStruct(shape, bf16), jax.ShapeDtypeStruct(shape, f32)),
        in_specs=[pl.BlockSpec(memory_space=pltpu.SMEM), vmem, vmem],
        out_specs=(vmem, vmem),
        compiler_params=pltpu.CompilerParams(vmem_limit_bytes=LIMIT),
        cost_estimate=pl.CostEstimate(
            flops=2 * X * TOK * ROWS * COLS, bytes_accessed=5 << 20, transcendentals=0
        ),
        name="feature_parts",
    )(place, grads, head)


def local(hidden_states, teacher_logprob, head_weight, token_ids, padding_mask):
    place = jnp.stack([lax.axis_index("x"), lax.axis_index("c")]).astype(jnp.int32)
    here, there = gather_hidden(hidden_states)
    teacher = teacher_logprob.reshape(Z * Y * C, 2, COLS // 2)
    teacher, there = lax.optimization_barrier((teacher, there))
    far, up, down, own, hidden_t = partial_logits(place, here, there, head_weight)
    teacher, own = lax.optimization_barrier((teacher, own))
    teacher = lax.all_to_all(teacher, ("z", "y", "c"), 0, 0, tiled=True).reshape(TOK, COLS)
    logits = add_far(own, shift(far, "x", X, 2)) + (shift(up, "x", X, 1) + shift(down, "x", X, 3))
    gap = logits - teacher.astype(f32)
    top = jnp.max(logits, axis=1)
    expo = jnp.exp(logits - top[:, None])
    stats = jnp.stack([top, jnp.sum(expo, axis=1), jnp.sum(expo * gap, axis=1)])
    stats = merge(spread(stats, ("y", "c"), Y * C))
    stats = merge(spread(stats, "z", Z))
    whole, total, weighted = stats[0], stats[1], stats[2]

    start = (
        (lax.axis_index("z") * Y + lax.axis_index("y")) * C + lax.axis_index("c")
    ) * COLS
    columns = start + jnp.arange(COLS, dtype=jnp.int32)
    onehot = (columns[None, :] == token_ids[:, None]).astype(f32)
    prob = jnp.exp(logits - whole[:, None]) / total[:, None]
    keep = padding_mask.astype(f32)[:, None]
    logit_grad = (
        keep * (prob * (gap - (weighted / total)[:, None]) + anchor_weight * (prob - onehot))
    ).astype(bf16)

    grads = spread(logit_grad, "x", X).reshape(X * TOK, COLS)
    sent, kept = feature_parts(place, grads, head_weight)
    pair = (kept + shift(sent, "c", C, 1).astype(f32)).astype(bf16)
    head_grad = jnp.dot(hidden_t, grads, preferred_element_type=f32).astype(bf16)
    pair, head_grad = lax.optimization_barrier((pair, head_grad))
    plane = lax.all_to_all(pair, ("x", "y"), 0, 0, tiled=True)
    plane = jnp.sum(plane.reshape(X, Y, K, FEAT, TOK).astype(f32), axis=1).astype(bf16)
    line = lax.all_to_all(plane.reshape(Z, FEAT, TOK), "z", 0, 0, tiled=True)
    hidden_grad = jnp.sum(line.astype(f32), axis=0).T

    return (logit_grad, hidden_grad, head_grad)


def solution(mesh):
    inner = Mesh(mesh.devices.reshape(X, Z, Y, C), ("x", "z", "y", "c"))
    v = ("z", "y", "c")
    in_specs = (P("x", v), P(("x",) + v, None), P("x", v), P("x"), P("x"))
    out_specs = (P("x", v), P("x", v), P("x", v))
    return jax.shard_map(local, mesh=inner, in_specs=in_specs, out_specs=out_specs, check_vma=False)
```

```python
import jax
import jax.numpy as jnp
from jax import lax
from jax.experimental import pallas as pl
from jax.experimental.pallas import tpu as pltpu
from jax.sharding import Mesh, PartitionSpec as P

anchor_weight = 0.25

X, Z, Y, C = 4, 16, 4, 2
K = Z // X
TOK = 128
FEAT = 32
ROWS = 1024
COLS = 1024
ADD_COST = 6 * 10**9
LIMIT = 48 * 1024 * 1024

f32 = jnp.float32
bf16 = jnp.bfloat16
STEPS = (2, 1, 3, 0)


def shift(value, axis, size, step):
    return lax.ppermute(value, axis, [(i, (i + step) % size) for i in range(size)])


def spread(value, axes, size):
    sent = jnp.broadcast_to(value[None], (size,) + value.shape)
    return lax.all_to_all(sent, axes, 0, 0, tiled=True)


def merge(parts):
    top = jnp.max(parts[:, 0], axis=0)
    scale = jnp.exp(parts[:, 0] - top[None])
    return jnp.stack(
        [top, jnp.sum(scale * parts[:, 1], axis=0), jnp.sum(scale * parts[:, 2], axis=0)]
    )


def gather_hidden(hidden_states):
    mine = spread(hidden_states.T, "z", Z)
    sent = jnp.broadcast_to(mine.reshape(X, 1, K, FEAT, TOK), (X, Y, K, FEAT, TOK))
    here = lax.all_to_all(sent.reshape(X * Y, K, FEAT, TOK), ("x", "y"), 0, 0, tiled=True)
    return here, shift(here, "c", C, 1)


def partial_kernel(place, here, there, head, far, up, down, own, hidden_t, lhs, flat, sem):
    me, core = place[0], place[1]
    outs = (far, up, down, own)
    for t in range(X):
        for k in range(K):
            for y in range(Y):
                row = (k * Y + y) * C * FEAT
                for mine, ref in ((core, here), (1 - core, there)):
                    at = pl.ds(pl.multiple_of(row + mine * FEAT, FEAT), FEAT)
                    piece = ref[t * Y + y, k]
                    lhs[t, at, :] = piece
                    flat[at, t * TOK : (t + 1) * TOK] = piece
    save = pltpu.make_async_copy(flat, hidden_t, sem)
    save.start()
    for step, out in zip(STEPS, outs):
        t = lax.rem(me + step, X)
        out[...] = lax.dot_general(
            lhs[t], head[...], (((0,), (0,)), ((), ())), preferred_element_type=f32
        )
    save.wait()


def partial_logits(place, here, there, head):
    vmem = pl.BlockSpec(memory_space=pltpu.VMEM)
    chunk = jax.ShapeDtypeStruct((TOK, COLS), f32)
    return pl.pallas_call(
        partial_kernel,
        out_shape=(chunk,) * X + (jax.ShapeDtypeStruct((ROWS, X * TOK), bf16),),
        in_specs=[pl.BlockSpec(memory_space=pltpu.SMEM), vmem, vmem, vmem],
        out_specs=(vmem,) * X + (pl.BlockSpec(memory_space=pl.ANY),),
        scratch_shapes=[
            pltpu.VMEM((X, ROWS, TOK), bf16),
            pltpu.VMEM((ROWS, X * TOK), bf16),
            pltpu.SemaphoreType.DMA,
        ],
        compiler_params=pltpu.CompilerParams(vmem_limit_bytes=LIMIT),
        cost_estimate=pl.CostEstimate(
            flops=2 * X * TOK * ROWS * COLS, bytes_accessed=6 << 20, transcendentals=0
        ),
        name="partial_logits",
    )(place, here, there, head)


def add_kernel(own, far, down, total):
    total[...] = own[...] + far[...] + down[...]


def add_far(own, far, down):
    rows = pl.BlockSpec((TOK // 2, COLS), lambda i: (i, 0))
    return pl.pallas_call(
        add_kernel,
        out_shape=jax.ShapeDtypeStruct((TOK, COLS), f32),
        grid=(2,),
        in_specs=[rows] * 3,
        out_specs=rows,
        compiler_params=pltpu.CompilerParams(vmem_limit_bytes=LIMIT),
        cost_estimate=pl.CostEstimate(flops=ADD_COST, bytes_accessed=3 << 19, transcendentals=0),
        name="add_far",
    )(own, far, down)


def feature_kernel(place, grads, head, sent, kept):
    first = place[1] == 0
    band = Y * C * FEAT
    for k in range(K):
        part = lax.dot_general(
            head[k * band : (k + 1) * band, :],
            grads[...],
            (((1,), (1,)), ((), ())),
            preferred_element_type=f32,
        )
        for y in range(Y):
            low = part[y * C * FEAT : y * C * FEAT + FEAT]
            high = part[y * C * FEAT + FEAT : (y + 1) * C * FEAT]
            keep = jnp.where(first, low, high)
            give = jnp.where(first, high, low).astype(bf16)
            for t in range(X):
                kept[t * Y + y, k] = keep[:, t * TOK : (t + 1) * TOK]
                sent[t * Y + y, k] = give[:, t * TOK : (t + 1) * TOK]


def feature_parts(place, grads, head):
    vmem = pl.BlockSpec(memory_space=pltpu.VMEM)
    shape = (X * Y, K, FEAT, TOK)
    return pl.pallas_call(
        feature_kernel,
        out_shape=(jax.ShapeDtypeStruct(shape, bf16), jax.ShapeDtypeStruct(shape, f32)),
        in_specs=[pl.BlockSpec(memory_space=pltpu.SMEM), vmem, vmem],
        out_specs=(vmem, vmem),
        compiler_params=pltpu.CompilerParams(vmem_limit_bytes=LIMIT),
        cost_estimate=pl.CostEstimate(
            flops=2 * X * TOK * ROWS * COLS, bytes_accessed=5 << 20, transcendentals=0
        ),
        name="feature_parts",
    )(place, grads, head)


def local(hidden_states, teacher_logprob, head_weight, token_ids, padding_mask):
    place = jnp.stack([lax.axis_index("x"), lax.axis_index("c")]).astype(jnp.int32)
    here, there = gather_hidden(hidden_states)
    teacher = teacher_logprob.reshape(Z * Y * C, 8, COLS // 8)
    teacher, there = lax.optimization_barrier((teacher, there))
    far, up, down, own, hidden_t = partial_logits(place, here, there, head_weight)
    teacher, own = lax.optimization_barrier((teacher, own))
    teacher = lax.all_to_all(teacher, ("z", "y", "c"), 0, 0, tiled=True).reshape(TOK, COLS)
    logits = add_far(own, shift(far, "x", X, 2), shift(down, "x", X, 3)) + shift(up, "x", X, 1)
    gap = logits - teacher.astype(f32)
    top = jnp.max(logits, axis=1)
    expo = jnp.exp(logits - top[:, None])
    stats = jnp.stack([top, jnp.sum(expo, axis=1), jnp.sum(expo * gap, axis=1)])
    stats = merge(spread(stats, ("y", "c"), Y * C))
    stats = merge(spread(stats, "z", Z))
    whole, total, weighted = stats[0], stats[1], stats[2]

    start = (
        (lax.axis_index("z") * Y + lax.axis_index("y")) * C + lax.axis_index("c")
    ) * COLS
    columns = start + jnp.arange(COLS, dtype=jnp.int32)
    onehot = (columns[None, :] == token_ids[:, None]).astype(f32)
    prob = jnp.exp(logits - whole[:, None]) / total[:, None]
    keep = padding_mask.astype(f32)[:, None]
    logit_grad = (
        keep * (prob * (gap - (weighted / total)[:, None]) + anchor_weight * (prob - onehot))
    ).astype(bf16)

    grads = spread(logit_grad, "x", X).reshape(X * TOK, COLS)
    sent, kept = feature_parts(place, grads, head_weight)
    pair = (kept + shift(sent, "c", C, 1).astype(f32)).astype(bf16)
    head_grad = jnp.dot(hidden_t, grads, preferred_element_type=f32).astype(bf16)
    pair, head_grad = lax.optimization_barrier((pair, head_grad))
    plane = lax.all_to_all(pair, ("x", "y"), 0, 0, tiled=True)
    plane = jnp.sum(plane.reshape(X, Y, K, FEAT, TOK).astype(f32), axis=1).astype(bf16)
    line = lax.all_to_all(plane.reshape(Z, FEAT, TOK), "z", 0, 0, tiled=True)
    hidden_grad = jnp.sum(line.astype(f32), axis=0).T

    return (logit_grad, hidden_grad, head_grad)


def solution(mesh):
    inner = Mesh(mesh.devices.reshape(X, Z, Y, C), ("x", "z", "y", "c"))
    v = ("z", "y", "c")
    in_specs = (P("x", v), P(("x",) + v, None), P("x", v), P("x"), P("x"))
    out_specs = (P("x", v), P("x", v), P("x", v))
    return jax.shard_map(local, mesh=inner, in_specs=in_specs, out_specs=out_specs, check_vma=False)
```

```python
import jax
import jax.numpy as jnp
from jax import lax
from jax.experimental import pallas as pl
from jax.experimental.pallas import tpu as pltpu
from jax.sharding import Mesh, PartitionSpec as P

anchor_weight = 0.25

X, Z, Y, C = 4, 16, 4, 2
K = Z // X
TOK = 128
FEAT = 32
ROWS = 1024
COLS = 1024
ADD_COST = 6 * 10**9
LIMIT = 48 * 1024 * 1024

f32 = jnp.float32
bf16 = jnp.bfloat16
STEPS = (2, 1, 3, 0)


def shift(value, axis, size, step):
    return lax.ppermute(value, axis, [(i, (i + step) % size) for i in range(size)])


def spread(value, axes, size):
    sent = jnp.broadcast_to(value[None], (size,) + value.shape)
    return lax.all_to_all(sent, axes, 0, 0, tiled=True)


def merge(parts):
    top = jnp.max(parts[:, 0], axis=0)
    scale = jnp.exp(parts[:, 0] - top[None])
    return jnp.stack(
        [top, jnp.sum(scale * parts[:, 1], axis=0), jnp.sum(scale * parts[:, 2], axis=0)]
    )


def gather_hidden(hidden_states):
    mine = spread(hidden_states.T, "z", Z)
    sent = jnp.broadcast_to(mine.reshape(X, 1, K, FEAT, TOK), (X, Y, K, FEAT, TOK))
    here = lax.all_to_all(sent.reshape(X * Y, K, FEAT, TOK), ("x", "y"), 0, 0, tiled=True)
    return here, shift(here, "c", C, 1)


def partial_kernel(place, here, there, head, far, up, down, own, hidden_t, lhs, flat, sem):
    me, core = place[0], place[1]
    outs = (far, up, down, own)
    for t in range(X):
        for k in range(K):
            for y in range(Y):
                row = (k * Y + y) * C * FEAT
                for mine, ref in ((core, here), (1 - core, there)):
                    at = pl.ds(pl.multiple_of(row + mine * FEAT, FEAT), FEAT)
                    piece = ref[t * Y + y, k]
                    lhs[t, at, :] = piece
                    flat[at, t * TOK : (t + 1) * TOK] = piece
    save = pltpu.make_async_copy(flat, hidden_t, sem)
    save.start()
    for step, out in zip(STEPS, outs):
        t = lax.rem(me + step, X)
        out[...] = lax.dot_general(
            lhs[t], head[...], (((0,), (0,)), ((), ())), preferred_element_type=f32
        )
    save.wait()


def partial_logits(place, here, there, head):
    vmem = pl.BlockSpec(memory_space=pltpu.VMEM)
    chunk = jax.ShapeDtypeStruct((TOK, COLS), f32)
    return pl.pallas_call(
        partial_kernel,
        out_shape=(chunk,) * X + (jax.ShapeDtypeStruct((ROWS, X * TOK), bf16),),
        in_specs=[pl.BlockSpec(memory_space=pltpu.SMEM), vmem, vmem, vmem],
        out_specs=(vmem,) * X + (pl.BlockSpec(memory_space=pl.ANY),),
        scratch_shapes=[
            pltpu.VMEM((X, ROWS, TOK), bf16),
            pltpu.VMEM((ROWS, X * TOK), bf16),
            pltpu.SemaphoreType.DMA,
        ],
        compiler_params=pltpu.CompilerParams(vmem_limit_bytes=LIMIT),
        cost_estimate=pl.CostEstimate(
            flops=2 * X * TOK * ROWS * COLS, bytes_accessed=6 << 20, transcendentals=0
        ),
        name="partial_logits",
    )(place, here, there, head)


def add_kernel(own, far, total):
    total[...] = own[...] + far[...]


def add_far(own, far):
    rows = pl.BlockSpec((TOK // 2, COLS), lambda i: (i, 0))
    return pl.pallas_call(
        add_kernel,
        out_shape=jax.ShapeDtypeStruct((TOK, COLS), f32),
        grid=(2,),
        in_specs=[rows, rows],
        out_specs=rows,
        compiler_params=pltpu.CompilerParams(vmem_limit_bytes=LIMIT),
        cost_estimate=pl.CostEstimate(flops=ADD_COST, bytes_accessed=3 << 19, transcendentals=0),
        name="add_far",
    )(own, far)


def feature_kernel(place, grads, head, sent, kept):
    first = place[1] == 0
    band = Y * C * FEAT
    for k in range(K):
        part = lax.dot_general(
            head[k * band : (k + 1) * band, :],
            grads[...],
            (((1,), (1,)), ((), ())),
            preferred_element_type=f32,
        )
        for y in range(Y):
            low = part[y * C * FEAT : y * C * FEAT + FEAT]
            high = part[y * C * FEAT + FEAT : (y + 1) * C * FEAT]
            keep = jnp.where(first, low, high)
            give = jnp.where(first, high, low).astype(bf16)
            for t in range(X):
                kept[t * Y + y, k] = keep[:, t * TOK : (t + 1) * TOK]
                sent[t * Y + y, k] = give[:, t * TOK : (t + 1) * TOK]


def feature_parts(place, grads, head):
    vmem = pl.BlockSpec(memory_space=pltpu.VMEM)
    shape = (X * Y, K, FEAT, TOK)
    return pl.pallas_call(
        feature_kernel,
        out_shape=(jax.ShapeDtypeStruct(shape, bf16), jax.ShapeDtypeStruct(shape, f32)),
        in_specs=[pl.BlockSpec(memory_space=pltpu.SMEM), vmem, vmem],
        out_specs=(vmem, vmem),
        compiler_params=pltpu.CompilerParams(vmem_limit_bytes=LIMIT),
        cost_estimate=pl.CostEstimate(
            flops=2 * X * TOK * ROWS * COLS, bytes_accessed=5 << 20, transcendentals=0
        ),
        name="feature_parts",
    )(place, grads, head)


def local(hidden_states, teacher_logprob, head_weight, token_ids, padding_mask):
    place = jnp.stack([lax.axis_index("x"), lax.axis_index("c")]).astype(jnp.int32)
    here, there = gather_hidden(hidden_states)
    teacher = teacher_logprob.reshape(Z * Y * C, 8, COLS // 8)
    teacher, there = lax.optimization_barrier((teacher, there))
    far, up, down, own, hidden_t = partial_logits(place, here, there, head_weight)
    teacher, own = lax.optimization_barrier((teacher, own))
    teacher = lax.all_to_all(teacher, ("z", "y", "c"), 0, 0, tiled=True).reshape(TOK, COLS)
    logits = add_far(own, shift(far, "x", X, 2)) + (shift(up, "x", X, 1) + shift(down, "x", X, 3))
    gap = logits - teacher.astype(f32)
    top = jnp.max(logits, axis=1)
    expo = jnp.exp(logits - top[:, None])
    stats = jnp.stack([top, jnp.sum(expo, axis=1), jnp.sum(expo * gap, axis=1)])
    stats = merge(spread(stats, ("y", "c"), Y * C))
    stats = merge(spread(stats, "z", Z))
    whole, total, weighted = stats[0], stats[1], stats[2]

    start = (
        (lax.axis_index("z") * Y + lax.axis_index("y")) * C + lax.axis_index("c")
    ) * COLS
    columns = start + jnp.arange(COLS, dtype=jnp.int32)
    onehot = (columns[None, :] == token_ids[:, None]).astype(f32)
    prob = jnp.exp(logits - whole[:, None]) / total[:, None]
    keep = padding_mask.astype(f32)[:, None]
    logit_grad = (
        keep * (prob * (gap - (weighted / total)[:, None]) + anchor_weight * (prob - onehot))
    ).astype(bf16)

    grads = spread(logit_grad, "x", X).reshape(X * TOK, COLS)
    sent, kept = feature_parts(place, grads, head_weight)
    pair = (kept + shift(sent, "c", C, 1).astype(f32)).astype(bf16)
    head_grad = jnp.dot(hidden_t, grads, preferred_element_type=f32).astype(bf16)
    pair, head_grad = lax.optimization_barrier((pair, head_grad))
    plane = lax.all_to_all(pair, ("x", "y"), 0, 0, tiled=True)
    plane = jnp.sum(plane.reshape(X, Y, K, FEAT, TOK).astype(f32), axis=1).astype(bf16)
    line = lax.all_to_all(plane.reshape(Z, FEAT, TOK), "z", 0, 0, tiled=True)
    hidden_grad = jnp.sum(line.astype(f32), axis=0).T

    return (logit_grad, hidden_grad, head_grad)


def solution(mesh):
    inner = Mesh(mesh.devices.reshape(X, Z, Y, C), ("x", "z", "y", "c"))
    v = ("z", "y", "c")
    in_specs = (P("x", v), P(("x",) + v, None), P("x", v), P("x"), P("x"))
    out_specs = (P("x", v), P("x", v), P("x", v))
    return jax.shard_map(local, mesh=inner, in_specs=in_specs, out_specs=out_specs, check_vma=False)
```
